128 devices in a mesh: node: 16 (over x, z), local: 8 (over y, core).
Axes of the slice: x: 4, y: 4, z: 4, core: 2. Of those that a mesh axis runs over, the one named last changes fastest.
Arguments:
- tokens: bfloat16 [4096, 3584], P(('node', 'local')), may hold values from -6 to 6
- gates: float32 [4096, 8], P(('node', 'local')), may hold values from 0.1 to 1
- routes: int32 [4096, 8], P(('node', 'local')), may hold values from 0 to 255, as said below
- hot_experts: int32 [8], replicated, may hold values from 0 to 127, as said below
- w_gate_up: bfloat16 [128, 3584, 2048], P(('node', 'local')), may hold values from -0.09375 to 0.09375
- w_down: bfloat16 [128, 1024, 3584], P(('node', 'local')), may hold values from -0.1875 to 0.1875
Outputs:
- combined: bfloat16 [4096, 3584], P(('node', 'local'))
The draws below stay inside these ranges and needn't reach their ends.
Inputs may be any that keep to these rules, and one draw needn't show every extreme that they name: hot_experts[l] % 8 == l, so the home device of hot_experts[l] has local index l; hot_experts[7] is 127 in every draw. `routes`: ids below 128 are home replicas (expert e lives on device e of node+local); id 128 + d is the spare slot of device d. Column k of a token names a replica of an expert e with e % 8 == k, so a token's experts are distinct. The rows of one device name any replica at most 2 times, and in every draw the home replica of each hot expert is named exactly 2 times by the rows of every device.
All inputs are finite; a program needn't handle non-finite values.
Results may differ from the reference program's by a relative error of at most 0.011.
Values may be sent and summed in bfloat16 or wider, within the bound.
No kernel may reach another device: no remote copies, remote signals or barrier semaphores. Data moves between devices by JAX's collectives and lax.ppermute only.
A program may use at most 192 MiB of HBM per device.

```python
import math
import jax
import jax.numpy as jnp
from jax import lax

D = 3584
FF = 1024
TOP = 8
TOK_DEV = 32
TOKENS = 4096
EXPERTS = 128
REPLICAS = 256
CAP = 2
N_NODE = 16
N_LOCAL = 8


def hot_table(key):
    node_key = jax.random.fold_in(key, 101)
    nodes = jax.random.randint(node_key, (N_LOCAL,), 0, N_NODE, dtype=jnp.int32)
    places = jnp.arange(N_LOCAL, dtype=jnp.int32)
    nodes = jnp.where(places == N_LOCAL - 1, N_NODE - 1, nodes).astype(jnp.int32)
    return nodes * N_LOCAL + places


def draw_hot_experts(key, part):
    return hot_table(key)


def draw_routes(key, part):
    hot = hot_table(key)
    key = jax.random.fold_in(key, 7)
    devices = N_NODE * N_LOCAL
    per_group = EXPERTS // TOP
    groups = jnp.arange(TOP, dtype=jnp.int32)[:, None]
    home_rep = jnp.arange(per_group, dtype=jnp.int32)[None, :] * TOP + groups
    home_hot = jnp.any(home_rep[:, :, None] == hot[None, None, :], axis=2)
    spare_expert = hot[jnp.arange(devices, dtype=jnp.int32) % N_LOCAL]
    spare_inside = (spare_expert % TOP)[None, :] == groups
    home_pos = jnp.repeat(home_rep, CAP, axis=1)
    spare_ids = jnp.repeat(EXPERTS + jnp.arange(devices, dtype=jnp.int32), CAP)
    spare_pos = jnp.broadcast_to(spare_ids[None, :], (TOP, devices * CAP))
    home_flag = jnp.repeat(home_hot, CAP, axis=1)
    spare_flag = jnp.repeat(spare_inside, CAP, axis=1)
    positions = jnp.concatenate([home_pos, spare_pos], axis=1)
    width_home = per_group * CAP
    total = positions.shape[1]
    home_index = jnp.arange(width_home, dtype=jnp.int32)[None, :] + groups * 0
    first_home = jnp.logical_and(home_index == 0, groups == 0)
    spare_index = jnp.arange(devices * CAP, dtype=jnp.int32)[None, :] + groups * 0
    last_spare = spare_index == (devices - 1) * CAP
    first_key, second_key = jax.random.split(key)
    noise = jax.random.randint(first_key, (devices, TOP, total), 0, 4096, dtype=jnp.int32)
    home_prio = jnp.where(home_flag[None], -5000, jnp.where(first_home[None], -4000, noise[:, :, :width_home]))
    spare_prio = jnp.where(spare_flag[None], jnp.where(last_spare[None], -4000, noise[:, :, width_home:] - 1024), 100000)
    prio = jnp.concatenate([home_prio, spare_prio], axis=2)
    scores = prio * total + jnp.arange(total, dtype=jnp.int32)[None, None, :]
    order = jnp.argsort(scores, axis=-1)[:, :, :TOK_DEV]
    chosen = jnp.take_along_axis(jnp.broadcast_to(positions[None], (devices, TOP, total)), order, axis=-1)
    shuffle = jax.random.randint(second_key, (devices, TOP, TOK_DEV), 0, 4096, dtype=jnp.int32) * TOK_DEV + jnp.arange(TOK_DEV, dtype=jnp.int32)
    permuted = jnp.argsort(shuffle, axis=-1)
    assigned = jnp.take_along_axis(chosen, permuted, axis=-1)
    return assigned.transpose(0, 2, 1).reshape(TOKENS, TOP).astype(jnp.int32)


def shard_levels(stream_key, shape, cuts, least, high):
    level, own = 1.0, jax.random.fold_in(stream_key, 6)
    for position, blocks in cuts:
        steps = jnp.exp(jax.random.uniform(jax.random.fold_in(own, position), (blocks,), jnp.float32, least / len(cuts), high / len(cuts)))
        level = level * jnp.repeat(steps, shape[position] // blocks).reshape([-1 if axis == position else 1 for axis in range(len(shape))])
    return level


def gaussian(rng, dims, scale, bound, cuts=(), kind=jnp.bfloat16):
    values = scale * jax.random.normal(rng, dims, jnp.float32)
    if cuts:
        values = values * shard_levels(rng, dims, cuts, -0.22, 0.18)
    return jnp.clip(values, -bound, bound).astype(kind)


def setup_inputs(seed: int = 0) -> dict:
    streams_of = jax.random.split(jax.random.key(seed), 7)
    tokens = gaussian(streams_of[0], (TOKENS, D), 1.0, 6.0, ((0, 128),))
    gates = jnp.clip(jnp.exp(math.log(1.0) - 2.3025851 * jax.random.uniform(streams_of[1], (TOKENS, TOP), jnp.float32) ** shard_levels(streams_of[1], (TOKENS, TOP), ((0, 128),), -0.2, 0.2)), 0.1, 1.0)
    routes = draw_routes(jax.random.fold_in(streams_of[6], 71), 0)
    hot_experts = draw_hot_experts(jax.random.fold_in(streams_of[6], 71), 0)
    w_gate_up = gaussian(streams_of[4], (EXPERTS, D, 2 * FF), D ** -0.5, 0.09375, ((0, 128),))
    w_down = gaussian(streams_of[5], (EXPERTS, FF, D), FF ** -0.5, 0.1875, ((0, 128),))
    return {"tokens": tokens, "gates": gates, "routes": routes, "hot_experts": hot_experts, "w_gate_up": w_gate_up, "w_down": w_down}


def expert_apply(rows, gate_up, down):
    both = jnp.dot(rows.astype(jnp.float32), gate_up.astype(jnp.float32), preferred_element_type=jnp.float32, precision=lax.Precision.HIGHEST)
    hidden = (jax.nn.silu(both[:, :FF]) * both[:, FF:]).astype(jnp.bfloat16)
    result = jnp.dot(hidden.astype(jnp.float32), down.astype(jnp.float32), preferred_element_type=jnp.float32, precision=lax.Precision.HIGHEST)
    return result.astype(jnp.bfloat16)


def reference(tokens, gates, routes, hot_experts, w_gate_up, w_down):
    devices = N_NODE * N_LOCAL
    block = TOK_DEV * TOP
    slots = devices * CAP
    blocks = routes.reshape(devices, block)
    same = blocks[:, :, None] == blocks[:, None, :]
    before = jnp.arange(block, dtype=jnp.int32)[None, :] < jnp.arange(block, dtype=jnp.int32)[:, None]
    rank = jnp.sum(jnp.logical_and(same, before[None]).astype(jnp.int32), axis=2)
    source = jnp.arange(devices, dtype=jnp.int32)[:, None]
    where_slot = (blocks * slots + source * CAP + rank).reshape(-1)
    table = jnp.full((REPLICAS * slots,), -1, jnp.int32).at[where_slot].set(jnp.arange(TOKENS * TOP, dtype=jnp.int32))
    flat_gates = gates.reshape(-1)

    def visit(total, replica):
        index = lax.dynamic_slice_in_dim(table, replica * slots, slots)
        valid = index >= 0
        safe = jnp.maximum(index, 0)
        spare_pick = hot_experts[jnp.maximum(replica - EXPERTS, 0) % N_LOCAL]
        expert = jnp.where(replica < EXPERTS, replica, spare_pick).astype(jnp.int32)
        rows = tokens[safe // TOP]
        outputs = expert_apply(rows, w_gate_up[expert], w_down[expert])
        weight = jnp.where(valid, flat_gates[safe], jnp.float32(0.0))
        total = total.at[safe // TOP].add(weight[:, None] * outputs.astype(jnp.float32))
        return total, None

    total, _ = lax.scan(visit, jnp.zeros((TOKENS, D), jnp.float32), jnp.arange(REPLICAS, dtype=jnp.int32))
    return total.astype(jnp.bfloat16)
```

```python
import functools

import jax
import jax.numpy as jnp
from jax import lax
from jax.experimental import pallas as pl
from jax.experimental.pallas import tpu as pltpu
from jax.sharding import PartitionSpec as P

LANES = 128
SIDE = 4
COLUMNS = 8
LAG = 2
DEPTH = 7
BLOCK = 512
UP = (7, 4)
DOWN = (2, 7)
UP_BLOCKS = UP[0] * UP[1] // 2
PARTS = ((UP_BLOCKS, UP_BLOCKS + 4), (UP_BLOCKS + 4, UP_BLOCKS + 7))
BLOCKS = UP_BLOCKS + DOWN[1]
STEPS = BLOCKS + LAG * (DEPTH - 1)
RANGES = ((0, UP_BLOCKS),) + PARTS
MIB = 1024 * 1024
DENSE = 57 * MIB
RELAY = 50 * MIB

HBM = pl.BlockSpec(memory_space=pltpu.HBM)
VMEM = pl.BlockSpec(memory_space=pltpu.VMEM)
SMEM = pl.BlockSpec(memory_space=pltpu.SMEM)


def hops():
    along_x, along_z = [], []
    for node in range(SIDE * SIDE):
        x, z = divmod(node, SIDE)
        for column in range(COLUMNS):
            turn = 1 if column % 2 == 0 else -1
            here = node * COLUMNS + column
            along_x.append((here, ((x + turn) % SIDE * SIDE + z) * COLUMNS + column))
            along_z.append((here, (x * SIDE + (z + turn) % SIDE) * COLUMNS + column))
    return along_x, along_z


def place(root):
    node = lax.axis_index("node")
    turn = jnp.where(lax.axis_index("local") % 2 == 0, 1, -1)
    a = jnp.mod(turn * (node // SIDE - root // SIDE), SIDE)
    b = jnp.mod(turn * (node % SIDE - root % SIDE), SIDE)
    is_root = jnp.logical_and(a == 0, b == 0)
    first_by_x = (a == 0) != (b == 0)
    first = jnp.where(jnp.logical_and(a == 0, b != 0), SIDE + b, a + b)
    second = jnp.where(jnp.logical_and(b == 0, a != 0), SIDE + a, a + b)
    first_by_x = jnp.logical_or(first_by_x, is_root)
    first, second = jnp.where(is_root, 1, first), jnp.where(is_root, 1, second)
    x_depth = jnp.where(first_by_x, first, second)
    z_depth = jnp.where(first_by_x, second, first)
    x_from_x = first_by_x == jnp.logical_or(b == 0, a == SIDE - 1)
    z_from_z = first_by_x == jnp.logical_or(a == 0, b == SIDE - 1)
    return jnp.stack([v.astype(jnp.int32) for v in (is_root, first_by_x, x_depth, z_depth, x_from_x, z_from_z)])


def own_block(own_up, own_down, tree, index):
    if index < UP_BLOCKS:
        row, column = divmod(tree * UP_BLOCKS + index, UP[1])
        return own_up.at[0, pl.ds(row * BLOCK, BLOCK), pl.ds(column * BLOCK, BLOCK)]
    column = index - UP_BLOCKS
    return own_down.at[0, pl.ds(tree * BLOCK, BLOCK), pl.ds(column * BLOCK, BLOCK)]


def home_of(held, kind, tree, index):
    if kind == 0:
        flat = tree * UP_BLOCKS + index
        row, column = flat // UP[1], flat % UP[1]
    else:
        row, column = tree, index - UP_BLOCKS
    row = pl.multiple_of(row * BLOCK, BLOCK)
    column = pl.multiple_of(column * BLOCK, BLOCK)
    return held.at[pl.ds(row, BLOCK), pl.ds(column, BLOCK)]


def touched(step):
    late = step - LAG
    return [
        kind
        for kind, (first, last) in enumerate(RANGES)
        if first <= step < last or (late >= first and late - LAG * (DEPTH - 1) < last)
    ]


def relay_kernel(step, count_old, fresh, info, own_up, own_down, *refs):
    kinds = touched(step)
    sending = step < STEPS
    old, rest = refs[:count_old], refs[count_old + len(kinds) - fresh :]
    sends, rest = (rest[:2], rest[2:]) if sending else ((), rest)
    held, (into, out_of) = rest[: len(kinds)], rest[len(kinds) :]
    is_root, is_other = info[0] == 1, info[0] == 0

    def store(source, lane, index, act):
        tree = jnp.where((info[1] == 1) == (lane == 0), 0, 1)
        for array, kind in zip(held, kinds):
            first, last = RANGES[kind]

            @pl.when(jnp.logical_and(index >= first, index < last))
            def _():
                act(pltpu.make_async_copy(source, home_of(array, kind, tree, index), out_of.at[lane]))

    def came(act):
        for lane in range(2):
            store(old[lane], lane, step - LAG - LAG * (info[2 + lane] - 1), act)

    if old:

        @pl.when(is_other)
        def _():
            came(lambda copy: copy.start())

    if step < BLOCKS:
        loads = [
            pltpu.make_async_copy(own_block(own_up, own_down, lane, step), sends[lane], into.at[lane])
            for lane in range(2)
        ]

        @pl.when(is_root if old else True)
        def _():
            for load in loads:
                load.start()
            for load in loads:
                load.wait()

        @pl.when(is_root)
        def _():
            for act in (lambda copy: copy.start(), lambda copy: copy.wait()):
                for lane in range(2):
                    store(sends[lane], lane, jnp.int32(step), act)

    if old and sending:
        for lane in range(2):
            straight = info[4 + lane] == 1
            for source, chosen in ((old[lane], straight), (old[1 - lane], jnp.logical_not(straight))):

                @pl.when(jnp.logical_and(is_other, chosen))
                def _():
                    sends[lane][...] = source[...]

    if old:

        @pl.when(is_other)
        def _():
            came(lambda copy: copy.wait())


def relay(step, info, own_up, own_down, old, held):
    kinds = touched(step)
    shapes = [(UP[0] * BLOCK, UP[1] * BLOCK)] + [(DOWN[0] * BLOCK, DOWN[1] * BLOCK)] * len(PARTS)
    block = jax.ShapeDtypeStruct((BLOCK, BLOCK), own_up.dtype)
    sends = [block, block] if step < STEPS else []
    known = [kind for kind in kinds if kind in held]
    assert known == kinds[: len(known)]
    begin = 3 + len(old)
    outs = pl.pallas_call(
        functools.partial(relay_kernel, step, len(old), len(kinds) - len(known)),
        out_shape=sends + [jax.ShapeDtypeStruct(shapes[kind], own_up.dtype) for kind in kinds],
        in_specs=[SMEM, HBM, HBM] + [VMEM] * len(old) + [HBM] * len(known),
        out_specs=[VMEM] * len(sends) + [HBM] * len(kinds),
        input_output_aliases={begin + i: len(sends) + i for i in range(len(known))},
        scratch_shapes=[pltpu.SemaphoreType.DMA((2,)), pltpu.SemaphoreType.DMA((2,))],
        compiler_params=pltpu.CompilerParams(vmem_limit_bytes=RELAY),
        cost_estimate=pl.CostEstimate(flops=0, bytes_accessed=8 * BLOCK * BLOCK, transcendentals=0),
        name="relay",
    )(info, own_up, own_down, *old, *[held[kind] for kind in known])
    held.update(zip(kinds, outs[len(sends) :]))
    return outs[: len(sends)]


def broadcast(info, own_up, own_down):
    along_x, along_z = hops()
    came, held = [], {}
    for step in range(STEPS + LAG):
        old = came[step - LAG] if step >= LAG else ()
        sends = relay(step, info, own_up, own_down, old, held)
        if sends:
            came.append([lax.ppermute(v, ("node", "local"), way) for v, way in zip(sends, (along_x, along_z))])
    return held


def up_kernel(rows, flags, gate_up, lift_up, hidden):
    gate = jnp.dot(rows[...], gate_up[...], preferred_element_type=jnp.float32)
    lift = jnp.dot(rows[...], lift_up[...], preferred_element_type=jnp.float32)
    value = gate / (1.0 + jnp.exp(-gate)) * lift
    hidden[...] = jnp.where(flags[...] > 0, value, 0.0).astype(hidden.dtype)


def up(rows, flags, weights):
    count, depth = rows.shape
    width = weights.shape[1] // 2
    tile = 256
    return pl.pallas_call(
        up_kernel,
        grid=(width // tile,),
        out_shape=jax.ShapeDtypeStruct((count, width), jnp.bfloat16),
        in_specs=[
            pl.BlockSpec((count, depth), lambda i: (0, 0)),
            pl.BlockSpec((count, 1), lambda i: (0, 0)),
            pl.BlockSpec((depth, tile), lambda i: (0, i)),
            pl.BlockSpec((depth, tile), lambda i: (0, i + width // tile)),
        ],
        out_specs=pl.BlockSpec((count, tile), lambda i: (0, i)),
        compiler_params=pltpu.CompilerParams(vmem_limit_bytes=DENSE),
        cost_estimate=pl.CostEstimate(
            flops=2 * count * weights.size, bytes_accessed=2 * weights.size, transcendentals=count * width
        ),
        name="up",
    )(rows, flags, weights, weights)


def down_kernel(hidden, weights, *refs):
    *kept, out = refs
    value = jnp.dot(hidden[...], weights[...], preferred_element_type=jnp.float32)
    if kept:
        flags, cold = kept
        value = jnp.where(flags[...] > 0, value, cold[...].astype(jnp.float32))
    out[...] = value.astype(out.dtype)


def down(hidden, weights, flags=None, cold=None, part=(UP_BLOCKS, BLOCKS)):
    count, depth = hidden.shape
    tile = BLOCK
    first, size = part[0] - UP_BLOCKS, part[1] - part[0]
    specs = [pl.BlockSpec((count, depth), lambda i: (0, 0)), pl.BlockSpec((depth, tile), lambda i: (0, i + first))]
    kept = ()
    if cold is not None:
        kept = (flags, cold)
        specs += [
            pl.BlockSpec((count, 1), lambda i: (0, 0)),
            pl.BlockSpec((count, tile), lambda i: (0, i + first)),
        ]
    return pl.pallas_call(
        down_kernel,
        grid=(size,),
        out_shape=jax.ShapeDtypeStruct((count, size * tile), jnp.bfloat16),
        in_specs=specs,
        out_specs=pl.BlockSpec((count, tile), lambda i: (0, i)),
        compiler_params=pltpu.CompilerParams(vmem_limit_bytes=DENSE),
        cost_estimate=pl.CostEstimate(
            flops=2 * hidden.size * size * tile, bytes_accessed=2 * depth * size * tile, transcendentals=0
        ),
        name="down",
    )(hidden, weights, *kept)


def local(tokens, gates, routes, hot_experts, w_gate_up, w_down):
    n_node = lax.axis_size("node")
    n_local = lax.axis_size("local")
    tok_dev, width = tokens.shape
    top = routes.shape[1]
    experts = n_node * n_local * w_gate_up.shape[0]
    column = lax.axis_index("local")
    hot = hot_experts[column]
    home_gate_up = w_gate_up[0]
    home_down = w_down[0]

    info = place(hot // n_local)
    held = broadcast(info, w_gate_up, w_down)

    ids = jnp.pad(routes.T.astype(jnp.bfloat16)[:, :, None], ((0, 0), (0, 0), (0, LANES - 1)))
    spread = jnp.concatenate(
        [jnp.broadcast_to(tokens[None], (n_local, tok_dev, width)), ids], axis=2
    ).reshape(n_local * tok_dev, width + LANES)
    node_tokens = lax.all_to_all(spread, "local", split_axis=0, concat_axis=0, tiled=True)
    rows = node_tokens[:, :width]
    replica = node_tokens[:, width].astype(jnp.int32)
    count_rows = rows.shape[0]
    is_hot = jnp.logical_or(replica >= experts, replica == hot)
    flags = is_hot.astype(jnp.float32)[:, None]

    target = jnp.where(is_hot, n_node, replica // n_local)
    row_ids = jnp.arange(count_rows, dtype=jnp.int32)
    same = target[:, None] == target[None, :]
    before = row_ids[None, :] < row_ids[:, None]
    rank = jnp.sum(jnp.logical_and(same, before).astype(jnp.int32), axis=1)
    per_node = 2 * n_local
    slot = jnp.where(is_hot, -1, target * per_node + rank)
    slot_ids = jnp.arange(n_node * per_node, dtype=jnp.int32)
    pick = (slot_ids[:, None] == slot[None, :]).astype(jnp.bfloat16)
    unpick = (slot[:, None] == slot_ids[None, :]).astype(jnp.bfloat16)
    outgoing = jnp.dot(pick, rows, preferred_element_type=jnp.float32).astype(jnp.bfloat16)
    received = lax.all_to_all(outgoing, "node", split_axis=0, concat_axis=0, tiled=True)
    cold_out = down(up(received, jnp.ones_like(flags), home_gate_up), home_down)
    returned = lax.all_to_all(cold_out, "node", split_axis=0, concat_axis=0, tiled=True)
    cold_rows = jnp.dot(unpick, returned, preferred_element_type=jnp.float32).astype(jnp.bfloat16)

    hidden = up(rows, flags, held[0])
    parts = []
    for kind, part in enumerate(PARTS, start=1):
        out = down(hidden, held[kind], flags, cold_rows, part)
        back = lax.all_to_all(out, "local", split_axis=0, concat_axis=0, tiled=True)
        back = back.reshape(top, tok_dev, out.shape[1]).astype(jnp.float32)
        parts.append(jnp.sum(gates.T[:, :, None] * back, axis=0).astype(jnp.bfloat16))
    return jnp.concatenate(parts, axis=1)


def solution(mesh):
    in_specs = (
        P(("node", "local"), None),
        P(("node", "local"), None),
        P(("node", "local"), None),
        P(),
        P(("node", "local"), None, None),
        P(("node", "local"), None, None),
    )
    out_specs = P(("node", "local"), None)
    return jax.shard_map(local, mesh=mesh, in_specs=in_specs, out_specs=out_specs, check_vma=False)
```

```python
import functools

import jax
import jax.numpy as jnp
from jax import lax
from jax.experimental import pallas as pl
from jax.experimental.pallas import tpu as pltpu
from jax.sharding import PartitionSpec as P

LANES = 128
SIDE = 4
COLUMNS = 8
LAG = 2
DEPTH = 7
PIECE = (256, 512)
UP = (7, 4)
DOWN = (2, 7)
UP_PIECES = UP[0] * UP[1]
PIECES = UP_PIECES + DOWN[0] * DOWN[1]
GROUP = 2
BLOCKS = PIECES // GROUP
BLOCK = (GROUP * PIECE[0], PIECE[1])
CUT = 4
PARTS = ((0, CUT), (CUT, DOWN[1]))
STEPS = BLOCKS + LAG * (DEPTH - 2)
RANGES = ((0, UP_PIECES),) + tuple((UP_PIECES + DOWN[0] * first, UP_PIECES + DOWN[0] * last) for first, last in PARTS)
MIB = 1024 * 1024
DEEP = 896
DENSE = 50 * MIB
RELAY = 50 * MIB

HBM = pl.BlockSpec(memory_space=pltpu.HBM)
VMEM = pl.BlockSpec(memory_space=pltpu.VMEM)
SMEM = pl.BlockSpec(memory_space=pltpu.SMEM)


def hops():
    along_x, along_z = [], []
    for node in range(SIDE * SIDE):
        x, z = divmod(node, SIDE)
        for column in range(COLUMNS):
            turn = 1 if column % 2 == 0 else -1
            here = node * COLUMNS + column
            along_x.append((here, ((x + turn) % SIDE * SIDE + z) * COLUMNS + column))
            along_z.append((here, (x * SIDE + (z + turn) % SIDE) * COLUMNS + column))
    return along_x, along_z


def place(hot):
    node, column = lax.axis_index("node"), lax.axis_index("local")
    root = hot[column] >> 3
    turn = 1 - 2 * (column & 1)
    a = (turn * ((node >> 2) - (root >> 2))) & 3
    b = (turn * ((node & 3) - (root & 3))) & 3
    is_root = jnp.logical_and(a == 0, b == 0)
    first_by_x = jnp.logical_or((a == 0) != (b == 0), is_root)
    depth = jnp.where(is_root, 1, a + b)
    first = jnp.where(jnp.logical_and(a == 0, b != 0), SIDE + b, depth)
    second = jnp.where(jnp.logical_and(b == 0, a != 0), SIDE + a, depth)
    depths = jnp.where(first_by_x, first, second), jnp.where(first_by_x, second, first)
    straight = (
        first_by_x == jnp.logical_or(b == 0, a == SIDE - 1),
        first_by_x == jnp.logical_or(a == 0, b == SIDE - 1),
    )
    return is_root, first_by_x, depths, straight


def spot(tree, piece):
    up = tree * UP[0] + piece % UP[0], piece // UP[0]
    rest = piece - UP_PIECES
    return up, (tree * DOWN[0] + rest % DOWN[0], rest // DOWN[0])


def window(array, row, column):
    rows, columns = PIECE
    return array.at[
        pl.ds(pl.multiple_of(row * rows, rows), rows), pl.ds(pl.multiple_of(column * columns, columns), columns)
    ]


def own_piece(own_up, own_down, tree, piece):
    up, rest = spot(tree, piece)
    return window(own_up.at[0], *up) if piece < UP_PIECES else window(own_down.at[0], *rest)


def home_of(held, kind, tree, piece):
    up, (row, column) = spot(tree, piece)
    if kind == 0:
        return window(held, *up)
    return window(held, row, column - PARTS[kind - 1][0])


def touched(step):
    late = step - LAG
    early = max(late - LAG * (DEPTH - 1), 0)
    return [
        kind
        for kind, (first, last) in enumerate(RANGES)
        if (step < BLOCKS and GROUP * step < last and GROUP * (step + 1) > first)
        or (late >= 0 and GROUP * early < last and GROUP * (late + 1) > first)
    ]


def relay_kernel(step, count_old, fresh, hot, own_up, own_down, *refs):
    kinds = touched(step)
    sending = step < STEPS
    old, rest = refs[:count_old], refs[count_old + len(kinds) - fresh :]
    sends, rest = (rest[:2], rest[2:]) if sending else ((), rest)
    held, (into, out_of) = rest[: len(kinds)], rest[len(kinds) :]
    is_root, first_by_x, depths, straight = place(hot)
    is_other = jnp.logical_not(is_root)

    def part(block, i):
        return block.at[pl.ds(i * PIECE[0], PIECE[0])]

    def store(source, lane, index, act):
        tree = jnp.where(first_by_x, lane, 1 - lane)
        again = jnp.logical_and(index >= BLOCKS, depths[1 - lane] == DEPTH)
        tree = jnp.where(again, 1 - tree, tree)
        index = jnp.where(again, index - LAG, index)
        for i in range(GROUP):
            piece = index * GROUP + i
            for array, kind in zip(held, kinds):
                first, last = RANGES[kind]

                @pl.when(jnp.logical_and(piece >= first, piece < last))
                def _():
                    copy = pltpu.make_async_copy(
                        part(source, i), home_of(array, kind, tree, jnp.maximum(piece, 0)), out_of.at[lane, i]
                    )
                    act(copy)

    def came(act):
        for lane in range(2):
            store(old[lane], lane, step - LAG - LAG * (depths[lane] - 1), act)

    if old:

        @pl.when(is_other)
        def _():
            came(lambda copy: copy.start())

    if step < BLOCKS + LAG:
        loads = [
            pltpu.make_async_copy(
                own_piece(own_up, own_down, tree, GROUP * index + i), part(sends[lane], i), into.at[lane, i]
            )
            for lane in range(2)
            for tree, index in (((lane, step) if step < BLOCKS else (1 - lane, step - LAG)),)
            for i in range(GROUP)
        ]

        @pl.when(is_root if old else True)
        def _():
            for load in loads:
                load.start()
            for load in loads:
                load.wait()

    if step < BLOCKS:

        @pl.when(is_root)
        def _():
            for act in (lambda copy: copy.start(), lambda copy: copy.wait()):
                for lane in range(2):
                    store(sends[lane], lane, jnp.int32(step), act)

    if old and sending:
        for lane in range(2):
            for source, chosen in ((old[lane], straight[lane]), (old[1 - lane], jnp.logical_not(straight[lane]))):

                @pl.when(jnp.logical_and(is_other, chosen))
                def _():
                    sends[lane][...] = source[...]

    if old:

        @pl.when(is_other)
        def _():
            came(lambda copy: copy.wait())


def relay(step, hot, own_up, own_down, old, held):
    kinds = touched(step)
    shapes = [own_up.shape[1:]] + [own_down.shape[1:]] * len(PARTS)
    block = jax.ShapeDtypeStruct(BLOCK, own_up.dtype)
    sends = [block, block] if step < STEPS else []
    known = [kind for kind in kinds if kind in held]
    assert known == kinds[: len(known)]
    begin = 3 + len(old)
    outs = pl.pallas_call(
        functools.partial(relay_kernel, step, len(old), len(kinds) - len(known)),
        out_shape=sends + [jax.ShapeDtypeStruct(shapes[kind], own_up.dtype) for kind in kinds],
        in_specs=[SMEM, HBM, HBM] + [VMEM] * len(old) + [HBM] * len(known),
        out_specs=[VMEM] * len(sends) + [HBM] * len(kinds),
        input_output_aliases={begin + i: len(sends) + i for i in range(len(known))},
        scratch_shapes=[pltpu.SemaphoreType.DMA((2, GROUP)), pltpu.SemaphoreType.DMA((2, GROUP))],
        compiler_params=pltpu.CompilerParams(vmem_limit_bytes=RELAY),
        cost_estimate=pl.CostEstimate(flops=0, bytes_accessed=8 * BLOCK[0] * BLOCK[1], transcendentals=0),
        name="relay",
    )(hot, own_up, own_down, *old, *[held[kind] for kind in known])
    held.update(zip(kinds, outs[len(sends) :]))
    return outs[: len(sends)]


def broadcast(hot, own_up, own_down):
    along_x, along_z = hops()
    came, held = [], {}
    for step in range(STEPS + LAG):
        old = came[step - LAG] if step >= LAG else ()
        sends = relay(step, hot, own_up, own_down, old, held)
        if sends:
            came.append([lax.ppermute(v, ("node", "local"), way) for v, way in zip(sends, (along_x, along_z))])
    return held


def up_kernel(rows, flags, weights, hidden, total):
    part = jnp.dot(rows[...], weights[...], preferred_element_type=jnp.float32)

    @pl.when(pl.program_id(0) == 0)
    def _():
        total[...] = part

    @pl.when(pl.program_id(0) > 0)
    def _():
        total[...] += part

    @pl.when(pl.program_id(0) == pl.num_programs(0) - 1)
    def _():
        width = hidden.shape[1]
        gate, lift = total[:, :width], total[:, width:]
        value = gate / (1.0 + jnp.exp(-gate)) * lift
        hidden[...] = jnp.where(flags[...] > 0, value, 0.0).astype(hidden.dtype)


def up(rows, flags, weights):
    count = rows.shape[0]
    depth, width = weights.shape
    tile = DEEP
    return pl.pallas_call(
        up_kernel,
        grid=(depth // tile,),
        out_shape=jax.ShapeDtypeStruct((count, width // 2), jnp.bfloat16),
        in_specs=[
            pl.BlockSpec((count, tile), lambda i: (0, i)),
            pl.BlockSpec((count, 1), lambda i: (0, 0)),
            pl.BlockSpec((tile, width), lambda i: (i, 0)),
        ],
        out_specs=pl.BlockSpec((count, width // 2), lambda i: (0, 0)),
        scratch_shapes=[pltpu.VMEM((count, width), jnp.float32)],
        compiler_params=pltpu.CompilerParams(vmem_limit_bytes=DENSE),
        cost_estimate=pl.CostEstimate(
            flops=2 * count * weights.size, bytes_accessed=2 * weights.size, transcendentals=count * width // 2
        ),
        name="up",
    )(rows, flags, weights)


def down_kernel(hidden, weights, *refs):
    *kept, out = refs
    value = jnp.dot(hidden[...], weights[...], preferred_element_type=jnp.float32)
    if kept:
        flags, cold = kept
        value = jnp.where(flags[...] > 0, value, cold[...].astype(jnp.float32))
    out[...] = value.astype(out.dtype)


def down(hidden, weights, tile, flags=None, cold=None):
    count, depth = hidden.shape
    width = weights.shape[1] if cold is None else cold.shape[1]
    specs = [pl.BlockSpec((count, depth), lambda i: (0, 0)), pl.BlockSpec((depth, tile), lambda i: (0, i))]
    kept = ()
    if cold is not None:
        kept = (flags, cold)
        specs += [pl.BlockSpec((count, 1), lambda i: (0, 0)), pl.BlockSpec((count, tile), lambda i: (0, i))]
    return pl.pallas_call(
        down_kernel,
        grid=(width // tile,),
        out_shape=jax.ShapeDtypeStruct((count, width), jnp.bfloat16),
        in_specs=specs,
        out_specs=pl.BlockSpec((count, tile), lambda i: (0, i)),
        compiler_params=pltpu.CompilerParams(vmem_limit_bytes=DENSE),
        cost_estimate=pl.CostEstimate(
            flops=2 * hidden.size * width, bytes_accessed=2 * depth * width, transcendentals=0
        ),
        name="down",
    )(hidden, weights, *kept)


def local(tokens, gates, routes, hot_experts, w_gate_up, w_down):
    n_node = lax.axis_size("node")
    n_local = lax.axis_size("local")
    tok_dev, width = tokens.shape
    top = routes.shape[1]
    experts = n_node * n_local * w_gate_up.shape[0]
    column = lax.axis_index("local")
    hot = hot_experts[column]
    home_gate_up = w_gate_up[0]
    home_down = w_down[0]

    held = broadcast(hot_experts, w_gate_up, w_down)

    ids = jnp.pad(routes.T.astype(jnp.bfloat16)[:, :, None], ((0, 0), (0, 0), (0, LANES - 1)))
    spread = jnp.concatenate(
        [jnp.broadcast_to(tokens[None], (n_local, tok_dev, width)), ids], axis=2
    ).reshape(n_local * tok_dev, width + LANES)
    rows = lax.all_to_all(spread, "local", split_axis=0, concat_axis=0, tiled=True)
    replica = rows[:, width].astype(jnp.int32)
    count_rows = rows.shape[0]
    is_hot = jnp.logical_or(replica >= experts, replica == hot)
    flags = is_hot.astype(jnp.float32)[:, None]

    target = jnp.where(is_hot, n_node, replica // n_local)
    row_ids = jnp.arange(count_rows, dtype=jnp.int32)
    same = target[:, None] == target[None, :]
    before = row_ids[None, :] < row_ids[:, None]
    rank = jnp.sum(jnp.logical_and(same, before).astype(jnp.int32), axis=1)
    per_node = 2 * n_local
    slot = jnp.where(is_hot, -1, target * per_node + rank)
    slot_ids = jnp.arange(n_node * per_node, dtype=jnp.int32)
    pick = (slot_ids[:, None] == slot[None, :]).astype(jnp.bfloat16)
    unpick = (slot[:, None] == slot_ids[None, :]).astype(jnp.bfloat16)
    outgoing = jnp.dot(pick, rows[:, :width], preferred_element_type=jnp.float32).astype(jnp.bfloat16)
    received = lax.all_to_all(outgoing, "node", split_axis=0, concat_axis=0, tiled=True)
    cold_out = down(up(received, jnp.ones_like(flags), home_gate_up), home_down, width // 2)
    returned = lax.all_to_all(cold_out, "node", split_axis=0, concat_axis=0, tiled=True)

    hidden = up(rows, flags, held[0])
    parts = []
    for kind, (first, last) in enumerate(PARTS, start=1):
        begin, end = first * PIECE[1], last * PIECE[1]
        cold = jnp.dot(unpick, returned[:, begin:end], preferred_element_type=jnp.float32).astype(jnp.bfloat16)
        out = down(hidden, held[kind], (end - begin) // 2, flags, cold)
        back = lax.all_to_all(out, "local", split_axis=0, concat_axis=0, tiled=True)
        back = back.reshape(top, tok_dev, out.shape[1]).astype(jnp.float32)
        parts.append(jnp.sum(gates.T[:, :, None] * back, axis=0).astype(jnp.bfloat16))
    return jnp.concatenate(parts, axis=1)


def solution(mesh):
    in_specs = (
        P(("node", "local"), None),
        P(("node", "local"), None),
        P(("node", "local"), None),
        P(),
        P(("node", "local"), None, None),
        P(("node", "local"), None, None),
    )
    out_specs = P(("node", "local"), None)
    return jax.shard_map(local, mesh=mesh, in_specs=in_specs, out_specs=out_specs, check_vma=False)
```
